512 devices in a mesh: seq: 256 (over z, y, x_hi, core), head: 2 (over x_lo).
Axes of the slice: x: 4 (x_hi: 2, x_lo: 2; x = x_hi * 2 + x_lo), y: 4, z: 16, core: 2. Of those that a mesh axis runs over, the one named last changes fastest.
Arguments:
- queries: bfloat16 [2, 262144, 128], P('head', 'seq'), may hold values from -88 to 88
- keys: bfloat16 [2, 262144, 128], P('head', 'seq'), may hold values from -4 to 4
- values: bfloat16 [2, 262144, 128], P('head', 'seq'), may hold values from -5 to 5
- out_grad: bfloat16 [2, 262144, 128], P('head', 'seq'), may hold values from -5 to 5
- route: int32 [2, 256], P('head', 'seq'), may hold values from 0 to 255, as said below
Outputs:
- attended: bfloat16 [2, 262144, 128], P('head', 'seq')
- query_grad: bfloat16 [2, 262144, 128], P('head', 'seq')
- key_grad: bfloat16 [2, 262144, 128], P('head', 'seq')
- value_grad: bfloat16 [2, 262144, 128], P('head', 'seq')
The draws below stay inside these ranges and needn't reach their ends.
Inputs may be any that keep to these rules, and one draw needn't show every extreme that they name: Bit s of route[h, j] equals bit s of route[h, j XOR 2^s], so partner is a permutation of the blocks for each head.
All inputs are finite; a program needn't handle non-finite values.
Results may differ from the reference program's by a relative error of at most 0.029.
Values may be sent and summed in bfloat16 or wider, within the bound.
No kernel may reach another device: no remote copies, remote signals or barrier semaphores. Data moves between devices by JAX's collectives and lax.ppermute only.
A program may use at most 64 MiB of HBM per device.

```python
import jax
import jax.numpy as jnp
from jax import lax

HEAD = 128
TOK_DEV = 1024
HEADS = 2
NBLK = 256
SEQ = 262144
SECTIONS = 8


def base_keys(key):
    return jnp.clip(jax.random.normal(key, (HEADS, SEQ, HEAD), jnp.float32), -4.0, 4.0)


def draw_keys(key, part):
    base = base_keys(key)
    return base.astype(jnp.bfloat16)


def draw_queries(key, part):
    key = jax.random.fold_in(key, 7)
    fresh = jnp.clip(jax.random.normal(key, (HEADS, SEQ, HEAD), jnp.float32), -5.0, 5.0)
    return fresh.astype(jnp.bfloat16)


def draw_route(key, part):
    key = jax.random.fold_in(key, 11)
    coins = jax.random.randint(key, (HEADS, SECTIONS, NBLK), 0, 2)
    blocks = jnp.arange(NBLK, dtype=jnp.int32)
    switches = jnp.zeros((HEADS, NBLK), jnp.int32)
    for level in range(SECTIONS):
        lower = blocks - blocks // 2 ** level % 2 * 2 ** level
        quiet = 6 - 6 // 2 ** level % 2 * 2 ** level
        chosen = coins[:, level, :][:, lower]
        chosen = jnp.where((lower == quiet)[None, :], 0, chosen)
        chosen = jnp.where((lower == 0)[None, :], 1, chosen)
        chosen = jnp.where((lower == NBLK - 1 - 2 ** level)[None, :], 1, chosen)
        switches = switches + chosen * 2 ** level
    return switches.astype(jnp.int32)


def block_scale(rng, dims, cuts, least, largest):
    def one(dim, blocks):
        heights = jax.random.uniform(jax.random.fold_in(jax.random.fold_in(rng, 6), dim), (blocks,), jnp.float32, least / len(cuts), largest / len(cuts))
        return jnp.repeat(jnp.exp(heights), dims[dim] // blocks).reshape((-1,) + (1,) * (len(dims) - dim - 1))

    level = one(*cuts[0])
    for cut in cuts[1:]:
        level = level * one(*cut)
    return level


def scatter_about(key, extent, deviation, reach, pieces=(), kind=jnp.bfloat16):
    entries = jax.random.normal(key, extent, jnp.float32) * deviation
    if len(pieces) > 0:
        entries = block_scale(key, extent, pieces, -0.22, 0.18) * entries
    return jnp.clip(entries, min=-reach, max=reach).astype(kind)


def setup_inputs(seed: int = 0) -> dict:
    key_of = jax.random.split(jax.random.key(seed), 6)
    queries = draw_queries(jax.random.fold_in(key_of[5], 71), 0)
    keys = draw_keys(jax.random.fold_in(key_of[5], 71), 0)
    values = scatter_about(key_of[2], (HEADS, SEQ, HEAD), 1.0, 5.0, ((0, 2), (1, 256)))
    out_grad = scatter_about(key_of[3], (HEADS, SEQ, HEAD), 1.0, 5.0, ((0, 2), (1, 256)))
    route = draw_route(jax.random.fold_in(key_of[5], 71), 0)
    return dict(queries=queries, keys=keys, values=values, out_grad=out_grad, route=route)


def round_bf(tensor):
    return lax.optimization_barrier(tensor.astype(jnp.bfloat16)).astype(jnp.float32)


def partner_blocks(switches):
    blocks = jnp.arange(NBLK, dtype=jnp.int32)
    holder = blocks
    for level in range(SECTIONS):
        taken = (switches // (2 ** level)) % 2
        across = holder[jnp.bitwise_xor(blocks, 2 ** level)]
        holder = jnp.where(taken == 1, across, holder)
    return holder


def allowed_cols(offset, count, rows_dev, leading):
    qpos = offset + jnp.arange(count)[:, None]
    kidx = jnp.arange(3 * rows_dev)[None, :]
    own_part = (kidx < rows_dev) & (kidx <= qpos)
    prev_part = (kidx >= rows_dev) & (kidx < 2 * rows_dev) & jnp.logical_not(leading)
    return own_part | prev_part | (kidx >= 2 * rows_dev)


def reference(queries, keys, values, out_grad, route):
    factor = HEAD ** -0.5
    attended_all, query_all, key_all, value_all = [], [], [], []
    for head_index in range(HEADS):
        query_blocks = queries[head_index].reshape(NBLK, TOK_DEV, HEAD)
        key_blocks = keys[head_index].reshape(NBLK, TOK_DEV, HEAD)
        value_blocks = values[head_index].reshape(NBLK, TOK_DEV, HEAD)
        grad_blocks = out_grad[head_index].reshape(NBLK, TOK_DEV, HEAD)
        partner = partner_blocks(route[head_index])

        def one_block(block):
            before = jnp.maximum(block - 1, 0)
            chosen = partner[block]
            query_rows = query_blocks[block].astype(jnp.float32)
            grad_rows = grad_blocks[block].astype(jnp.float32)
            keys_all = jnp.concatenate([key_blocks[block], key_blocks[before], key_blocks[chosen]], 0).astype(jnp.float32)
            values_all = jnp.concatenate([value_blocks[block], value_blocks[before], value_blocks[chosen]], 0).astype(jnp.float32)
            scores = jnp.einsum("qd,kd->qk", query_rows, keys_all) * factor
            allowed = allowed_cols(0, TOK_DEV, TOK_DEV, block == 0)
            scores = jnp.where(allowed, scores, -jnp.inf)
            peak = jnp.max(scores, -1, keepdims=True)
            log_total = peak[:, 0] + jnp.log(jnp.sum(jnp.exp(scores - peak), -1))
            weights = round_bf(jnp.exp(scores - log_total[:, None]))
            attended = jnp.einsum("qk,kd->qd", weights, values_all).astype(jnp.bfloat16)
            correction = jnp.sum(grad_rows * attended.astype(jnp.float32), -1)
            pushed = jnp.einsum("qd,kd->qk", grad_rows, values_all)
            shaped = round_bf(weights * (pushed - correction[:, None]))
            query_grad = (jnp.einsum("qk,kd->qd", shaped, keys_all) * factor).astype(jnp.bfloat16)
            key_terms = jnp.einsum("qk,qd->kd", shaped, query_rows) * factor
            value_terms = jnp.einsum("qk,qd->kd", weights, grad_rows)
            return attended, query_grad, key_terms, value_terms

        attended, query_grad, key_terms, value_terms = lax.map(one_block, jnp.arange(NBLK, dtype=jnp.int32))

        def assemble(terms):
            own_terms = terms[:, :TOK_DEV]
            prev_terms = round_bf(terms[:, TOK_DEV:2 * TOK_DEV])
            shifted = jnp.concatenate([prev_terms[1:], jnp.zeros((1, TOK_DEV, HEAD), jnp.float32)], 0)
            part_terms = round_bf(terms[:, 2 * TOK_DEV:])
            placed = jnp.zeros_like(part_terms).at[partner].set(part_terms)
            return (own_terms + shifted + placed).astype(jnp.bfloat16).reshape(SEQ, HEAD)

        attended_all.append(attended.reshape(SEQ, HEAD))
        query_all.append(query_grad.reshape(SEQ, HEAD))
        key_all.append(assemble(key_terms))
        value_all.append(assemble(value_terms))
    return (jnp.stack(attended_all), jnp.stack(query_all), jnp.stack(key_all), jnp.stack(value_all))
```

```python
import functools
import math

import jax
import jax.numpy as jnp
from jax import lax
from jax.experimental import pallas as pl
from jax.experimental.pallas import tpu as pltpu
from jax.sharding import PartitionSpec as P

F32 = jnp.float32
BF16 = jnp.bfloat16
NT = (((1,), (1,)), ((), ()))
NN = (((1,), (0,)), ((), ()))
CHUNK = 256
INF = float("inf")
VMEM_LIMIT = 48 * 1024 * 1024


def dot(a, b, dims=NN):
    return lax.dot_general(a, b, dims, preferred_element_type=F32)


def chunks(rows):
    return [slice(at, at + CHUNK) for at in range(0, rows, CHUNK)]


def causal(scores, first):
    kpos = lax.broadcasted_iota(jnp.int32, scores.shape, 0)
    qpos = lax.broadcasted_iota(jnp.int32, scores.shape, 1) + first
    return jnp.where(kpos <= qpos, scores, -INF)


def call(kernel, out_shape, n_in, scalars=0):
    vmem = pl.BlockSpec(memory_space=pltpu.VMEM)
    smem = pl.BlockSpec(memory_space=pltpu.SMEM)
    return pl.pallas_call(
        kernel,
        out_shape=out_shape,
        in_specs=[smem] * scalars + [vmem] * n_in,
        out_specs=jax.tree.map(lambda _: vmem, out_shape),
        compiler_params=pltpu.CompilerParams(vmem_limit_bytes=VMEM_LIMIT),
    )


def thirds(x):
    high = x.astype(BF16).astype(F32)
    middle = (x - high).astype(BF16).astype(F32)
    return high, middle, x - high - middle


def stats_kernel(scale, at, route, q_ref, g_ref, k_ref, v_ref, kb_ref, vb_ref, out_ref, notes_ref, rows_ref):
    leading = at[0] == 0
    parts = q_ref.shape[0] // CHUNK
    rows_ref[...] = jnp.full(rows_ref.shape, route[0].astype(F32))
    for t, cols in enumerate(chunks(q_ref.shape[0])):
        q, g = q_ref[cols], g_ref[cols]
        own = causal(dot(k_ref[: cols.stop], q, NT) * scale, cols.start)
        before = dot(kb_ref[...], q, NT) * scale
        peak_before = jnp.where(leading, -INF, jnp.max(before, 0, keepdims=True))
        peak = jnp.maximum(jnp.max(own, 0, keepdims=True), peak_before)
        own = jnp.exp2(own - peak)
        before = jnp.exp2(before - jnp.where(leading, INF, peak))
        total = jnp.sum(own, 0, keepdims=True) + jnp.sum(before, 0, keepdims=True)
        pushed = jnp.sum(own * dot(v_ref[: cols.stop], g, NT), 0, keepdims=True)
        pushed += jnp.sum(before * dot(vb_ref[...], g, NT), 0, keepdims=True)
        for kind, row in enumerate((peak + jnp.log2(total), pushed / total)):
            out_ref[kind : kind + 1, cols] = row
            for i, third in enumerate(thirds(row)):
                to = (3 * kind + i) * parts + t
                rows_ref[to : to + 1] = third
    notes_ref[...] = rows_ref[...].T.astype(BF16)


def read_notes(notes_ref, parts):
    rows = notes_ref[...].astype(F32).T
    sums = [sum(rows[(3 * kind + i) * parts : (3 * kind + i + 1) * parts] for i in range(3)) for kind in range(2)]
    return [[total[t : t + 1] for t in range(parts)] for total in sums]


def joined(elsewhere, scores):
    peak = jnp.max(scores, 0, keepdims=True)
    raw = jnp.exp2(scores - peak)
    here = peak + jnp.log2(jnp.sum(raw, 0, keepdims=True))
    top = jnp.maximum(elsewhere, here)
    log_total = top + jnp.log2(jnp.exp2(elsewhere - top) + jnp.exp2(here - top))
    return raw * jnp.exp2(peak - log_total), log_total, jnp.exp2(elsewhere - log_total)


def query_kernel(
    scale, factor, at, q_ref, g_ref, k_ref, v_ref, kb_ref, vb_ref, kp_ref, vp_ref, stats_ref,
    att_ref, dq_ref, dk_ref, dv_ref, dkb_ref, dvb_ref, dkb_acc, dvb_acc,
):
    leading = at[0] == 0
    k_t, kb_t, kp_t = k_ref[...].T, kb_ref[...].T, kp_ref[...].T
    v_t, vb_t, vp_t = v_ref[...].T, vb_ref[...].T, vp_ref[...].T
    dk_ref[...] = jnp.zeros_like(dk_ref)
    dv_ref[...] = jnp.zeros_like(dv_ref)
    dkb_acc[...] = jnp.zeros_like(dkb_acc)
    dvb_acc[...] = jnp.zeros_like(dvb_acc)
    for cols in chunks(q_ref.shape[0]):
        q, g = q_ref[cols], g_ref[cols]
        keys = slice(0, cols.stop)
        w_partner, log_total, _ = joined(stats_ref[0:1, cols], dot(kp_ref[...], q, NT) * scale)
        w_partner = w_partner.astype(BF16)
        w_own = jnp.exp2(causal(dot(k_ref[keys], q, NT) * scale, cols.start) - log_total).astype(BF16)
        log_before = jnp.where(leading, INF, log_total)
        w_before = jnp.exp2(dot(kb_ref[...], q, NT) * scale - log_before).astype(BF16)
        attended = dot(vp_t, w_partner) + dot(v_t[:, keys], w_own) + dot(vb_t, w_before)
        attended = attended.astype(BF16).astype(F32)
        att_ref[cols] = attended.T.astype(BF16)
        drift = jnp.sum(attended * g.astype(F32).T, 0, keepdims=True)

        def shape(weights, v):
            return (weights.astype(F32) * (dot(v, g, NT) - drift)).astype(BF16)

        s_before = shape(w_before, vb_ref[...])
        dkb_acc[...] += dot(s_before, q)
        dvb_acc[...] += dot(w_before, g)
        s_own = shape(w_own, v_ref[keys])
        dk_ref[keys] += dot(s_own, q)
        dv_ref[keys] += dot(w_own, g)
        s_partner = shape(w_partner, vp_ref[...])
        dq = dot(kp_t, s_partner) + dot(k_t[:, keys], s_own) + dot(kb_t, s_before)
        dq_ref[cols] = (dq * factor).T.astype(BF16)
    dk_ref[...] *= factor
    dkb_ref[...] = (dkb_acc[...] * factor).astype(BF16)
    dvb_ref[...] = dvb_acc[...].astype(BF16)


def key_kernel(scale, factor, q_ref, g_ref, k_ref, v_ref, notes_ref, dk_own, dv_own, dk_ref, dv_ref, dk_acc, dv_acc):
    dk_acc[...] = jnp.zeros_like(dk_acc)
    dv_acc[...] = jnp.zeros_like(dv_acc)
    elsewhere, pushed_there = read_notes(notes_ref, q_ref.shape[0] // CHUNK)
    for t, cols in enumerate(chunks(q_ref.shape[0])):
        q, g = q_ref[cols], g_ref[cols]
        weights, _, share = joined(elsewhere[t], dot(k_ref[...], q, NT) * scale)
        pushed = dot(v_ref[...], g, NT)
        drift = share * pushed_there[t] + jnp.sum(weights * pushed, 0, keepdims=True)
        weights = weights.astype(BF16)
        shaped = (weights.astype(F32) * (pushed - drift)).astype(BF16)
        dk_acc[...] += dot(shaped, q)
        dv_acc[...] += dot(weights, g)
    dk_ref[...] = dk_own[...] + (dk_acc[...] * factor).astype(BF16).astype(F32)
    dv_ref[...] = dv_own[...] + dv_acc[...].astype(BF16).astype(F32)


def partner_kernel(route_ref, partner_ref, inverse_ref):
    route = route_ref[...]
    n = route.shape[1]
    lane = lax.broadcasted_iota(jnp.int32, route.shape, 1)

    def section(holder, s):
        far = 1 << s
        across = jnp.where((lane >> s) & 1 == 1, pltpu.roll(holder, far, 1), pltpu.roll(holder, n - far, 1))
        return jnp.where((route >> s) & 1 == 1, across, holder)

    sections = range(n.bit_length() - 1)
    partner_ref[...] = functools.reduce(section, sections, lane)
    inverse_ref[...] = functools.reduce(section, reversed(sections), lane)


def reorder_kernel(partner_ref, inverse_ref, x_ref, out_ref):
    keep = x_ref.shape[1] // 2

    def body(d, carry):
        out_ref[d, :keep] = x_ref[partner_ref[0, d], :keep]
        out_ref[d, keep:] = x_ref[inverse_ref[0, d], keep:]
        return carry

    lax.fori_loop(0, x_ref.shape[0], body, 0, unroll=8)


def shifted(x, distance):
    n = lax.axis_size("seq")
    return lax.ppermute(x, "seq", [(i, i + distance) for i in range(n) if 0 <= i + distance < n])


def local(queries, keys, values, out_grad, route):
    q, k, v, g = queries[0], keys[0], values[0], out_grad[0]
    rows, width = q.shape
    n = lax.axis_size("seq")
    me = lax.axis_index("seq")
    factor = width**-0.5
    scale = factor * math.log2(math.e)
    at = me.reshape(1)
    part = 2 * rows // n
    block = jax.ShapeDtypeStruct((rows, width), BF16)
    block32 = jax.ShapeDtypeStruct((rows, width), F32)

    vmem = pl.BlockSpec(memory_space=pltpu.VMEM)
    smem = pl.BlockSpec(memory_space=pltpu.SMEM)
    params = pltpu.CompilerParams(vmem_limit_bytes=VMEM_LIMIT)

    k_before, v_before = shifted((k, v), 1)
    stats, notes = pl.pallas_call(
        functools.partial(stats_kernel, scale),
        out_shape=(jax.ShapeDtypeStruct((2, rows), F32), jax.ShapeDtypeStruct((n, width), BF16)),
        in_specs=[smem] * 2 + [vmem] * 6,
        out_specs=(vmem, vmem),
        scratch_shapes=[pltpu.VMEM((width, n), F32)],
        compiler_params=params,
    )(at, route.reshape(1), q, g, k, v, k_before, v_before)

    def pairs(x):
        return x.reshape(n, -1, 2, width)

    spread = jnp.concatenate(
        [
            pairs(jnp.concatenate([k, v])),
            pairs(jnp.concatenate([q, g])),
            pairs(jnp.stack([notes, notes], 1)),
        ],
        1,
    )
    spread = lax.all_to_all(spread, "seq", 0, 0, tiled=True)
    routes = spread[:, -1, 0, -1].astype(jnp.int32).reshape(1, n)
    index = jax.ShapeDtypeStruct((1, n), jnp.int32)
    partner, inverse = call(partner_kernel, (index, index), 1)(routes)
    moved = call(reorder_kernel, jax.ShapeDtypeStruct(spread.shape, BF16), 1, 2)(partner, inverse, spread)
    moved = lax.all_to_all(moved, "seq", 0, 0, tiled=True)
    kv = moved[:, : part // 2].reshape(2 * rows, width)
    qg = moved[:, part // 2 : part].reshape(2 * rows, width)
    notes = moved[:, -1, 0]

    acc = [pltpu.VMEM((rows, width), F32)] * 2
    attended, query_grad, dk, dv, dk_before, dv_before = pl.pallas_call(
        functools.partial(query_kernel, scale, factor),
        out_shape=(block, block, block32, block32, block, block),
        in_specs=[smem] + [vmem] * 9,
        out_specs=(vmem,) * 6,
        scratch_shapes=acc,
        compiler_params=params,
    )(at, q, g, k, v, k_before, v_before, kv[:rows], kv[rows:], stats)
    dk_back, dv_back = shifted((dk_before, dv_before), -1)
    dk, dv = pl.pallas_call(
        functools.partial(key_kernel, scale, factor),
        out_shape=(block32, block32),
        in_specs=[vmem] * 7,
        out_specs=(vmem,) * 2,
        scratch_shapes=acc,
        compiler_params=params,
    )(qg[:rows], qg[rows:], k, v, notes, dk, dv)
    key_grad = (dk + dk_back.astype(F32)).astype(BF16)
    value_grad = (dv + dv_back.astype(F32)).astype(BF16)
    return attended[None], query_grad[None], key_grad[None], value_grad[None]


def solution(mesh):
    whole = P("head", "seq", None)
    return jax.shard_map(
        local,
        mesh=mesh,
        in_specs=(whole,) * 4 + (P("head", "seq"),),
        out_specs=(whole,) * 4,
        check_vma=False,
    )
```

```python
import functools
import math

import jax
import jax.numpy as jnp
from jax import lax
from jax.experimental import pallas as pl
from jax.experimental.pallas import tpu as pltpu
from jax.sharding import PartitionSpec as P

F32 = jnp.float32
BF16 = jnp.bfloat16
NT = (((1,), (1,)), ((), ()))
NN = (((1,), (0,)), ((), ()))
CHUNK = 256
LONG = 1024
INF = float("inf")
VMEM_LIMIT = 32 * 1024 * 1024


def dot(a, b, dims=NN):
    return lax.dot_general(a, b, dims, preferred_element_type=F32)


def chunks(rows, size=CHUNK):
    return [slice(at, at + size) for at in range(0, rows, size)]


def causal(scores, first):
    kpos = lax.broadcasted_iota(jnp.int32, scores.shape, 0)
    qpos = lax.broadcasted_iota(jnp.int32, scores.shape, 1) + first
    return jnp.where(kpos <= qpos, scores, -INF)


def call(kernel, out_shape, n_in, scalars=0):
    vmem = pl.BlockSpec(memory_space=pltpu.VMEM)
    smem = pl.BlockSpec(memory_space=pltpu.SMEM)
    return pl.pallas_call(
        kernel,
        out_shape=out_shape,
        in_specs=[smem] * scalars + [vmem] * n_in,
        out_specs=jax.tree.map(lambda _: vmem, out_shape),
        compiler_params=pltpu.CompilerParams(vmem_limit_bytes=VMEM_LIMIT),
    )


def thirds(x):
    high = x.astype(BF16).astype(F32)
    middle = (x - high).astype(BF16).astype(F32)
    return high, middle, x - high - middle


def stats_kernel(
    scale, at, route, q_ref, g_ref, k_ref, v_ref, before_ref, own_pairs, swapped_pairs, q_pairs, g_pairs,
    out_ref, notes_ref, spread_ref, rows_ref, sems,
):
    leading = at[0] == 0
    half = own_pairs.shape[1]
    middle = q_pairs.shape[0]
    swap = route[0] & 1 == 1
    kv_to = spread_ref.at[:, :half]
    copies = [
        pltpu.make_async_copy(q_pairs, spread_ref.at[:middle, half : 2 * half], sems.at[0]),
        pltpu.make_async_copy(g_pairs, spread_ref.at[middle:, half : 2 * half], sems.at[1]),
    ]
    for copy in copies:
        copy.start()

    @pl.when(swap)
    def _():
        pltpu.make_async_copy(swapped_pairs, kv_to, sems.at[2]).start()

    @pl.when(jnp.logical_not(swap))
    def _():
        pltpu.make_async_copy(own_pairs, kv_to, sems.at[2]).start()

    rows = k_ref.shape[0]
    kb_ref, vb_ref = before_ref.at[:rows], before_ref.at[rows:]
    places = rows_ref.shape[1]
    parts = q_ref.shape[0] // places
    rows_ref[...] = jnp.full(rows_ref.shape, route[0].astype(F32))
    for cols in chunks(q_ref.shape[0]):
        q, g = q_ref[cols], g_ref[cols]
        own = causal(dot(k_ref[: cols.stop], q, NT) * scale, cols.start)
        before = dot(kb_ref[...], q, NT) * scale
        peak_before = jnp.where(leading, -INF, jnp.max(before, 0, keepdims=True))
        peak = jnp.maximum(jnp.max(own, 0, keepdims=True), peak_before)
        own = jnp.exp2(own - peak)
        before = jnp.exp2(before - jnp.where(leading, INF, peak))
        total = jnp.sum(own, 0, keepdims=True) + jnp.sum(before, 0, keepdims=True)
        pushed = jnp.sum(own * dot(v_ref[: cols.stop], g, NT), 0, keepdims=True)
        pushed += jnp.sum(before * dot(vb_ref[...], g, NT), 0, keepdims=True)
        for kind, row in enumerate((peak + jnp.log2(total), pushed / total)):
            out_ref[kind : kind + 1, cols] = row
            for i, third in enumerate(thirds(row)):
                for at_row in range(0, CHUNK, places):
                    to = (3 * kind + i) * parts + (cols.start + at_row) // places
                    rows_ref[to : to + 1] = third[:, at_row : at_row + places]
    notes_ref[...] = rows_ref[...].T.astype(BF16)
    for copy in copies:
        copy.wait()
    pltpu.make_async_copy(own_pairs, kv_to, sems.at[2]).wait()


def read_notes(notes_ref, count):
    rows = notes_ref[...].astype(F32).T
    parts = count // rows.shape[1]
    per = parts * LONG // count
    sums = [sum(rows[(3 * kind + i) * parts : (3 * kind + i + 1) * parts] for i in range(3)) for kind in range(2)]
    return [
        [jnp.concatenate([total[t : t + 1] for t in range(at, at + per)], 1) for at in range(0, parts, per)]
        for total in sums
    ]


def joined(elsewhere, scores):
    peak = jnp.max(scores, 0, keepdims=True)
    raw = jnp.exp2(scores - peak)
    here = peak + jnp.log2(jnp.sum(raw, 0, keepdims=True))
    top = jnp.maximum(elsewhere, here)
    log_total = top + jnp.log2(jnp.exp2(elsewhere - top) + jnp.exp2(here - top))
    return raw * jnp.exp2(peak - log_total), log_total, jnp.exp2(elsewhere - log_total)


def local_kernel(
    scale, at, q_ref, g_ref, k_ref, v_ref, before_ref, stats_ref,
    out_ref, shaped_keys_ref, keys_ref, so_ref, wo_ref, g_t_ref,
):
    leading = at[0] == 0
    rows = k_ref.shape[0]
    kb_ref, vb_ref = before_ref.at[:rows], before_ref.at[rows:]
    g_t_ref[...] = g_ref[...].T
    k_t, kb_t = k_ref[...].T, kb_ref[...].T
    v_t, vb_t = v_ref[...].T, vb_ref[...].T
    for cols in chunks(q_ref.shape[0]):
        q, g = q_ref[cols], g_ref[cols]
        keys = slice(0, cols.stop)
        total, drift = stats_ref[0:1, cols], stats_ref[1:2, cols]

        def shape(weights, v):
            return (weights.astype(F32) * (dot(v, g, NT) - drift)).astype(BF16)

        wo = jnp.exp2(causal(dot(k_ref[keys], q, NT) * scale, cols.start) - total).astype(BF16)
        so = shape(wo, v_ref[keys])
        wb = jnp.exp2(dot(kb_ref[...], q, NT) * scale - jnp.where(leading, INF, total)).astype(BF16)
        sb = shape(wb, vb_ref[...])
        out_ref[:, cols] = dot(v_t[:, keys], wo) + dot(vb_t, wb)
        shaped_keys_ref[:, cols] = dot(k_t[:, keys], so) + dot(kb_t, sb)
        keys_ref[:, cols] = dot(k_t[:, keys], wo) + dot(kb_t, wb)
        wo_ref[keys, cols] = wo
        so_ref[keys, cols] = so


def next_kernel(scale, qg_ref, k_ref, v_ref, stats_ref, s_ref, w_ref):
    rows = k_ref.shape[0]
    q_ref, g_ref = qg_ref.at[:rows], qg_ref.at[rows:]
    for cols in chunks(rows):
        weights = jnp.exp2(dot(k_ref[...], q_ref[cols], NT) * scale - stats_ref[0:1, cols]).astype(BF16)
        pushed = dot(v_ref[...], g_ref[cols], NT)
        w_ref[:, cols] = weights
        s_ref[:, cols] = (weights.astype(F32) * (pushed - stats_ref[1:2, cols])).astype(BF16)


def scaled(q, g, shares_ref):
    down = jnp.concatenate([shares_ref[...]] * 4, 0).T
    share, delta = down[:, 0:1], down[:, 1:2]
    q, g = q.astype(F32), g.astype(F32)
    return (q * share).astype(BF16), jnp.concatenate([(q * delta).astype(BF16), (g * share).astype(BF16)], 1)


def query_kernel(
    scale, factor, q_ref, g_ref, partner_ref, stats_ref, out_ref, shaped_keys_ref, keys_ref, g_t_ref,
    att_ref, dq_ref, shares_ref,
):
    rows = q_ref.shape[0]
    kp_ref, vp_ref = partner_ref.at[:rows], partner_ref.at[rows:]
    kp_t, vp_t = kp_ref[...].T, vp_ref[...].T
    for cols in chunks(rows, LONG):
        q, g = q_ref[cols], g_ref[cols]
        weights, _, share = joined(stats_ref[0:1, cols], dot(kp_ref[...], q, NT) * scale)
        weights = weights.astype(BF16)
        attended = (dot(vp_t, weights) + share * out_ref[:, cols]).astype(BF16).astype(F32)
        att_ref[cols] = attended.T.astype(BF16)
        drift = jnp.sum(attended * g_t_ref[:, cols].astype(F32), 0, keepdims=True)
        delta = share * (stats_ref[1:2, cols] - drift)
        shaped = (weights.astype(F32) * (dot(vp_ref[...], g, NT) - drift)).astype(BF16)
        dq = dot(kp_t, shaped) + share * shaped_keys_ref[:, cols] + delta * keys_ref[:, cols]
        dq_ref[cols] = (dq * factor).T.astype(BF16)
        shares_ref[0:1, cols] = share
        shares_ref[1:2, cols] = delta


def partner_terms_kernel(scale, factor, qg_ref, k_ref, v_ref, notes_ref, dk_ref, dv_ref, s_ref, w_ref):
    rows = k_ref.shape[0]
    q_ref, g_ref = qg_ref.at[:rows], qg_ref.at[rows:]
    elsewhere, pushed_there = read_notes(notes_ref, rows)
    for t, cols in enumerate(chunks(rows, LONG)):
        q, g = q_ref[cols], g_ref[cols]
        weights, _, share = joined(elsewhere[t], dot(k_ref[...], q, NT) * scale)
        pushed = dot(v_ref[...], g, NT)
        drift = share * pushed_there[t] + jnp.sum(weights * pushed, 0, keepdims=True)
        weights = weights.astype(BF16)
        s_ref[:, cols] = (weights.astype(F32) * (pushed - drift)).astype(BF16)
        w_ref[:, cols] = weights
    dk_ref[...] = (dot(s_ref[...], q_ref[...]) * factor).astype(BF16)
    dv_ref[...] = dot(w_ref[...], g_ref[...]).astype(BF16)


def sum_kernel(
    factor, q_ref, g_ref, qg_next_ref, shares_ref, shares_next_ref, so_ref, wo_ref, sn_ref, wn_ref, dkp_ref, dvp_ref,
    dk_ref, dv_ref, key_x, both_x, next_key_x, next_both_x,
):
    rows, width = q_ref.shape
    key_x[...], both_x[...] = scaled(q_ref[...], g_ref[...], shares_ref)
    next_key_x[...], next_both_x[...] = scaled(qg_next_ref[:rows], qg_next_ref[rows:], shares_next_ref)
    for keys in chunks(rows):
        later = slice(keys.start, rows)
        both = dot(wn_ref[keys], next_both_x[...])
        dk = (dot(sn_ref[keys], next_key_x[...]) + both[:, :width]) * factor
        dk = dk.astype(BF16).astype(F32) + dkp_ref[keys].astype(F32)
        dv = both[:, width:].astype(BF16).astype(F32) + dvp_ref[keys].astype(F32)
        both = dot(wo_ref[keys, later], both_x[later])
        dk_ref[keys] = (dk + (dot(so_ref[keys, later], key_x[later]) + both[:, :width]) * factor).astype(BF16)
        dv_ref[keys] = (dv + both[:, width:]).astype(BF16)


def partner_kernel(notes_ref, partner_ref, inverse_ref):
    n = partner_ref.shape[1]
    route = (notes_ref[...].astype(F32).T[-1:]).astype(jnp.int32) >> 1
    lane = lax.broadcasted_iota(jnp.int32, route.shape, 1)

    def section(holder, s):
        far = 1 << s
        across = jnp.where((lane >> s) & 1 == 1, pltpu.roll(holder, far, 1), pltpu.roll(holder, n - far, 1))
        return jnp.where((route >> s) & 1 == 1, across, holder)

    sections = range(n.bit_length() - 1)
    partner_ref[...] = functools.reduce(section, sections, lane)
    inverse_ref[...] = functools.reduce(section, reversed(sections), lane)


def reorder_kernel(partner_ref, inverse_ref, x_ref, out_ref):
    keep = x_ref.shape[1] // 2

    def body(d, carry):
        out_ref[d, :keep] = x_ref[partner_ref[0, d], :keep]
        out_ref[d, keep:] = x_ref[inverse_ref[0, d], keep:]
        return carry

    lax.fori_loop(0, x_ref.shape[0], body, 0, unroll=8)


def shifted(x, distance):
    n = lax.axis_size("seq")
    return lax.ppermute(x, "seq", [(i, i + distance) for i in range(n) if 0 <= i + distance < n])


def swapped(x):
    return lax.ppermute(x, "seq", [(i, i ^ 1) for i in range(lax.axis_size("seq"))])


def exchange(x):
    groups = [list(range(core, lax.axis_size("seq"), 2)) for core in range(2)]
    return lax.all_to_all(x, "seq", 0, 0, axis_index_groups=groups, tiled=True)


def local(queries, keys, values, out_grad, route):
    q, k, v, g = queries[0], keys[0], values[0], out_grad[0]
    rows, width = q.shape
    n = lax.axis_size("seq")
    me = lax.axis_index("seq")
    factor = width**-0.5
    scale = factor * math.log2(math.e)
    at = me.reshape(1)
    places = n // 2
    part = 2 * rows // places
    swap = (route[0, 0] & 1) == 1
    block = jax.ShapeDtypeStruct((rows, width), BF16)

    vmem = pl.BlockSpec(memory_space=pltpu.VMEM)
    smem = pl.BlockSpec(memory_space=pltpu.SMEM)
    params = pltpu.CompilerParams(vmem_limit_bytes=VMEM_LIMIT)

    kv_own = jnp.concatenate([k, v])
    kv_before = shifted(kv_own, 1)
    kv_swapped = swapped(kv_own)

    def pairs(x):
        return x.reshape(-1, part // 2, 2, width)

    anywhere = pl.BlockSpec(memory_space=pl.ANY)
    stats, notes, spread = pl.pallas_call(
        functools.partial(stats_kernel, scale),
        out_shape=(
            jax.ShapeDtypeStruct((2, rows), F32),
            jax.ShapeDtypeStruct((places, width), BF16),
            jax.ShapeDtypeStruct((places, part + 1, 2, width), BF16),
        ),
        in_specs=[smem] * 2 + [vmem] * 5 + [anywhere] * 4,
        out_specs=(vmem, vmem, anywhere),
        scratch_shapes=[pltpu.VMEM((width, places), F32), pltpu.SemaphoreType.DMA((3,))],
        compiler_params=params,
    )(at, route.reshape(1), q, g, k, v, kv_before, pairs(kv_own), pairs(kv_swapped), pairs(q), pairs(g))
    spread = spread.at[:, part].set(jnp.broadcast_to(notes[:, None], (places, 2, width)))
    spread = exchange(spread)
    square = jax.ShapeDtypeStruct((rows, rows), BF16)
    across32 = jax.ShapeDtypeStruct((width, rows), F32)
    from_local = pl.pallas_call(
        functools.partial(local_kernel, scale),
        out_shape=(across32,) * 3 + (square,) * 2 + (jax.ShapeDtypeStruct((width, rows), BF16),),
        in_specs=[smem] + [vmem] * 6,
        out_specs=(vmem,) * 6,
        compiler_params=params,
    )(at, q, g, k, v, kv_before, stats)
    qg_next, stats_next = shifted((jnp.concatenate([q, g]), stats), -1)
    spread, from_local, qg_next, stats_next = lax.optimization_barrier((spread, from_local, qg_next, stats_next))
    out, shaped_keys, weighted_keys, so, wo, g_t = from_local
    index = jax.ShapeDtypeStruct((1, places), jnp.int32)
    partner, inverse = call(partner_kernel, (index, index), 1)(spread[:, -1, 0])
    moved = call(reorder_kernel, jax.ShapeDtypeStruct(spread.shape, BF16), 1, 2)(partner, inverse, spread)
    moved = exchange(moved)
    from_next = pl.pallas_call(
        functools.partial(next_kernel, scale),
        out_shape=(square,) * 2,
        in_specs=[vmem] * 4,
        out_specs=(vmem,) * 2,
        compiler_params=params,
    )(qg_next, k, v, stats_next)
    moved, from_next = lax.optimization_barrier((moved, from_next))
    sn, wn = from_next
    kv = moved[:, : part // 2].reshape(2 * rows, width)
    rest = moved[:, part // 2 :]
    rest = jnp.where(swap, swapped(rest), rest)
    qg = rest[:, : part // 2].reshape(2 * rows, width)
    notes = rest[:, -1, 0]

    attended, query_grad, shares = pl.pallas_call(
        functools.partial(query_kernel, scale, factor),
        out_shape=(block, block, jax.ShapeDtypeStruct((2, rows), F32)),
        in_specs=[vmem] * 8,
        out_specs=(vmem,) * 3,
        compiler_params=params,
    )(q, g, kv, stats, out, shaped_keys, weighted_keys, g_t)
    shares_next = shifted(shares, -1)
    dk, dv = pl.pallas_call(
        functools.partial(partner_terms_kernel, scale, factor),
        out_shape=(block, block),
        in_specs=[vmem] * 4,
        out_specs=(vmem,) * 2,
        scratch_shapes=[pltpu.VMEM((rows, rows), BF16)] * 2,
        compiler_params=params,
    )(qg, k, v, notes)
    one, two = pltpu.VMEM((rows, width), BF16), pltpu.VMEM((rows, 2 * width), BF16)
    key_grad, value_grad = pl.pallas_call(
        functools.partial(sum_kernel, factor),
        out_shape=(block, block),
        in_specs=[vmem] * 11,
        out_specs=(vmem,) * 2,
        scratch_shapes=[one, two, one, two],
        compiler_params=params,
    )(q, g, qg_next, shares, shares_next, so, wo, sn, wn, dk, dv)
    return attended[None], query_grad[None], key_grad[None], value_grad[None]


def solution(mesh):
    whole = P("head", "seq", None)
    return jax.shard_map(
        local,
        mesh=mesh,
        in_specs=(whole,) * 4 + (P("head", "seq"),),
        out_specs=(whole,) * 4,
        check_vma=False,
    )
```

```python
import functools
import math

import jax
import jax.numpy as jnp
from jax import lax
from jax.experimental import pallas as pl
from jax.experimental.layout import Layout, with_layout_constraint
from jax.experimental.pallas import tpu as pltpu
from jax.sharding import PartitionSpec as P

F32 = jnp.float32
BF16 = jnp.bfloat16
NT = (((1,), (1,)), ((), ()))
NN = (((1,), (0,)), ((), ()))
CHUNK = 256
MIDDLE = 512
LONG = 1024
INF = float("inf")
VMEM_LIMIT = 16 * 1024 * 1024


def dot(a, b, dims=NN):
    return lax.dot_general(a, b, dims, preferred_element_type=F32)


def chunks(rows, size=CHUNK):
    return [slice(at, at + size) for at in range(0, rows, size)]


def causal(scores, first):
    kpos = lax.broadcasted_iota(jnp.int32, scores.shape, 0)
    qpos = lax.broadcasted_iota(jnp.int32, scores.shape, 1) + first
    return jnp.where(kpos <= qpos, scores, -INF)


def call(kernel, out_shape, n_in, scalars=0):
    vmem = pl.BlockSpec(memory_space=pltpu.VMEM)
    smem = pl.BlockSpec(memory_space=pltpu.SMEM)
    return pl.pallas_call(
        kernel,
        out_shape=out_shape,
        in_specs=[smem] * scalars + [vmem] * n_in,
        out_specs=jax.tree.map(lambda _: vmem, out_shape),
        compiler_params=pltpu.CompilerParams(vmem_limit_bytes=VMEM_LIMIT),
    )


def thirds(x):
    high = x.astype(BF16).astype(F32)
    middle = (x - high).astype(BF16).astype(F32)
    return high, middle, x - high - middle


def own_kernel(scale, q_ref, g_ref, k_ref, v_ref, out_ref):
    for cols in chunks(q_ref.shape[0]):
        q, g = q_ref[cols], g_ref[cols]
        own = causal(dot(k_ref[: cols.stop], q, NT) * scale, cols.start)
        peak = jnp.max(own, 0, keepdims=True)
        own = jnp.exp2(own - peak)
        out_ref[0:1, cols] = peak
        out_ref[1:2, cols] = jnp.sum(own, 0, keepdims=True)
        out_ref[2:3, cols] = jnp.sum(own * dot(v_ref[: cols.stop], g, NT), 0, keepdims=True)


def stats_kernel(
    scale, at, route, q_ref, g_ref, own_ref, before_ref, own_pairs, swapped_pairs, q_pairs, g_pairs,
    out_ref, notes_ref, spread_ref, rows_ref, sems,
):
    leading = at[0] == 0
    half = own_pairs.shape[1]
    middle = q_pairs.shape[0]
    swap = route[0] & 1 == 1
    kv_to = spread_ref.at[:, :half]
    copies = [
        pltpu.make_async_copy(q_pairs, spread_ref.at[:middle, half : 2 * half], sems.at[0]),
        pltpu.make_async_copy(g_pairs, spread_ref.at[middle:, half : 2 * half], sems.at[1]),
    ]
    for copy in copies:
        copy.start()

    @pl.when(swap)
    def _():
        pltpu.make_async_copy(swapped_pairs, kv_to, sems.at[2]).start()

    @pl.when(jnp.logical_not(swap))
    def _():
        pltpu.make_async_copy(own_pairs, kv_to, sems.at[2]).start()

    rows = q_ref.shape[0]
    kb_ref, vb_ref = before_ref.at[:rows], before_ref.at[rows:]
    places = rows_ref.shape[1]
    parts = q_ref.shape[0] // places
    rows_ref[...] = jnp.full(rows_ref.shape, route[0].astype(F32))
    for cols in chunks(rows, MIDDLE):
        q, g = q_ref[cols], g_ref[cols]
        before = dot(kb_ref[...], q, NT) * scale
        peak_own = own_ref[0:1, cols]
        peak = jnp.maximum(peak_own, jnp.where(leading, -INF, jnp.max(before, 0, keepdims=True)))
        before = jnp.exp2(before - jnp.where(leading, INF, peak))
        share = jnp.exp2(peak_own - peak)
        total = share * own_ref[1:2, cols] + jnp.sum(before, 0, keepdims=True)
        pushed = share * own_ref[2:3, cols] + jnp.sum(before * dot(vb_ref[...], g, NT), 0, keepdims=True)
        for kind, row in enumerate((peak + jnp.log2(total), pushed / total)):
            out_ref[kind : kind + 1, cols] = row
            for i, third in enumerate(thirds(row)):
                for at_row in range(0, MIDDLE, places):
                    to = (3 * kind + i) * parts + (cols.start + at_row) // places
                    rows_ref[to : to + 1] = third[:, at_row : at_row + places]
    notes_ref[...] = rows_ref[...].T.astype(BF16)
    for copy in copies:
        copy.wait()
    pltpu.make_async_copy(own_pairs, kv_to, sems.at[2]).wait()


def read_notes(notes_ref, count):
    rows = notes_ref[...].astype(F32).T
    parts = count // rows.shape[1]
    per = parts * LONG // count
    sums = [sum(rows[(3 * kind + i) * parts : (3 * kind + i + 1) * parts] for i in range(3)) for kind in range(2)]
    return [
        [jnp.concatenate([total[t : t + 1] for t in range(at, at + per)], 1) for at in range(0, parts, per)]
        for total in sums
    ]


def joined(elsewhere, scores):
    peak = jnp.max(scores, 0, keepdims=True)
    raw = jnp.exp2(scores - peak)
    here = peak + jnp.log2(jnp.sum(raw, 0, keepdims=True))
    top = jnp.maximum(elsewhere, here)
    log_total = top + jnp.log2(jnp.exp2(elsewhere - top) + jnp.exp2(here - top))
    return raw * jnp.exp2(peak - log_total), log_total, jnp.exp2(elsewhere - log_total)


def local_kernel(
    scale, at, q_ref, g_ref, k_ref, v_ref, before_ref, stats_ref,
    out_ref, shaped_keys_ref, keys_ref, so_ref, wo_ref, g_t_ref,
):
    leading = at[0] == 0
    rows = k_ref.shape[0]
    kb_ref, vb_ref = before_ref.at[:rows], before_ref.at[rows:]
    g_t_ref[...] = g_ref[...].T
    k_t, kb_t = k_ref[...].T, kb_ref[...].T
    v_t, vb_t = v_ref[...].T, vb_ref[...].T
    for cols in chunks(q_ref.shape[0]):
        q, g = q_ref[cols], g_ref[cols]
        keys = slice(0, cols.stop)
        total, drift = stats_ref[0:1, cols], stats_ref[1:2, cols]

        def shape(weights, v):
            return (weights.astype(F32) * (dot(v, g, NT) - drift)).astype(BF16)

        wo = jnp.exp2(causal(dot(k_ref[keys], q, NT) * scale, cols.start) - total).astype(BF16)
        so = shape(wo, v_ref[keys])
        wb = jnp.exp2(dot(kb_ref[...], q, NT) * scale - jnp.where(leading, INF, total)).astype(BF16)
        sb = shape(wb, vb_ref[...])
        out_ref[:, cols] = dot(v_t[:, keys], wo) + dot(vb_t, wb)
        shaped_keys_ref[:, cols] = dot(k_t[:, keys], so) + dot(kb_t, sb)
        keys_ref[:, cols] = dot(k_t[:, keys], wo) + dot(kb_t, wb)
        wo_ref[keys, cols] = wo
        so_ref[keys, cols] = so


def next_kernel(scale, qg_ref, k_ref, v_ref, stats_ref, s_ref, w_ref):
    rows = k_ref.shape[0]
    q_ref, g_ref = qg_ref.at[:rows], qg_ref.at[rows:]
    for cols in chunks(rows):
        weights = jnp.exp2(dot(k_ref[...], q_ref[cols], NT) * scale - stats_ref[0:1, cols]).astype(BF16)
        pushed = dot(v_ref[...], g_ref[cols], NT)
        w_ref[:, cols] = weights
        s_ref[:, cols] = (weights.astype(F32) * (pushed - stats_ref[1:2, cols])).astype(BF16)


def scaled(q, g, shares_ref):
    down = jnp.concatenate([shares_ref[...]] * 4, 0).T
    share, delta = down[:, 0:1], down[:, 1:2]
    q, g = q.astype(F32), g.astype(F32)
    return (q * share).astype(BF16), jnp.concatenate([(q * delta).astype(BF16), (g * share).astype(BF16)], 1)


def query_kernel(
    scale, factor, q_ref, g_ref, partner_ref, stats_ref, out_ref, shaped_keys_ref, keys_ref, g_t_ref,
    att_ref, dq_ref, shares_ref,
):
    rows = q_ref.shape[0]
    kp_ref, vp_ref = partner_ref.at[:rows], partner_ref.at[rows:]
    kp_t, vp_t = kp_ref[...].T, vp_ref[...].T
    for cols in chunks(rows, LONG):
        q, g = q_ref[cols], g_ref[cols]
        weights, _, share = joined(stats_ref[0:1, cols], dot(kp_ref[...], q, NT) * scale)
        weights = weights.astype(BF16)
        attended = (dot(vp_t, weights) + share * out_ref[:, cols]).astype(BF16).astype(F32)
        att_ref[cols] = attended.T.astype(BF16)
        drift = jnp.sum(attended * g_t_ref[:, cols].astype(F32), 0, keepdims=True)
        delta = share * (stats_ref[1:2, cols] - drift)
        shaped = (weights.astype(F32) * (dot(vp_ref[...], g, NT) - drift)).astype(BF16)
        dq = dot(kp_t, shaped) + share * shaped_keys_ref[:, cols] + delta * keys_ref[:, cols]
        dq_ref[cols] = (dq * factor).T.astype(BF16)
        shares_ref[0:1, cols] = share
        shares_ref[1:2, cols] = delta


def partner_terms_kernel(scale, factor, qg_ref, k_ref, v_ref, notes_ref, dk_ref, dv_ref, s_ref, w_ref):
    rows = k_ref.shape[0]
    q_ref, g_ref = qg_ref.at[:rows], qg_ref.at[rows:]
    elsewhere, pushed_there = read_notes(notes_ref, rows)
    for t, cols in enumerate(chunks(rows, LONG)):
        q, g = q_ref[cols], g_ref[cols]
        weights, _, share = joined(elsewhere[t], dot(k_ref[...], q, NT) * scale)
        pushed = dot(v_ref[...], g, NT)
        drift = share * pushed_there[t] + jnp.sum(weights * pushed, 0, keepdims=True)
        weights = weights.astype(BF16)
        s_ref[:, cols] = (weights.astype(F32) * (pushed - drift)).astype(BF16)
        w_ref[:, cols] = weights
    dk_ref[...] = (dot(s_ref[...], q_ref[...]) * factor).astype(BF16)
    dv_ref[...] = dot(w_ref[...], g_ref[...]).astype(BF16)


def sum_kernel(
    factor, q_ref, g_ref, qg_next_ref, shares_ref, shares_next_ref, so_ref, wo_ref, sn_ref, wn_ref, dkp_ref, dvp_ref,
    dk_ref, dv_ref, key_x, both_x, next_key_x, next_both_x,
):
    rows, width = q_ref.shape
    key_x[...], both_x[...] = scaled(q_ref[...], g_ref[...], shares_ref)
    next_key_x[...], next_both_x[...] = scaled(qg_next_ref[:rows], qg_next_ref[rows:], shares_next_ref)
    for keys in chunks(rows):
        later = slice(keys.start, rows)
        both = dot(wn_ref[keys], next_both_x[...])
        dk = (dot(sn_ref[keys], next_key_x[...]) + both[:, :width]) * factor
        dk = dk.astype(BF16).astype(F32) + dkp_ref[keys].astype(F32)
        dv = both[:, width:].astype(BF16).astype(F32) + dvp_ref[keys].astype(F32)
        both = dot(wo_ref[keys, later], both_x[later])
        dk_ref[keys] = (dk + (dot(so_ref[keys, later], key_x[later]) + both[:, :width]) * factor).astype(BF16)
        dv_ref[keys] = (dv + both[:, width:]).astype(BF16)


def partner_kernel(notes_ref, partner_ref, inverse_ref):
    n = partner_ref.shape[1]
    route = (notes_ref[...].astype(F32).T[-1:]).astype(jnp.int32) >> 1
    lane = lax.broadcasted_iota(jnp.int32, route.shape, 1)

    def section(holder, s):
        far = 1 << s
        across = jnp.where((lane >> s) & 1 == 1, pltpu.roll(holder, far, 1), pltpu.roll(holder, n - far, 1))
        return jnp.where((route >> s) & 1 == 1, across, holder)

    sections = range(n.bit_length() - 1)
    partner_ref[...] = functools.reduce(section, sections, lane)
    inverse_ref[...] = functools.reduce(section, reversed(sections), lane)


def reorder_kernel(partner_ref, inverse_ref, x_ref, out_ref):
    keep = x_ref.shape[1] // 2

    def body(d, carry):
        out_ref[d, :keep] = x_ref[partner_ref[0, d], :keep]
        out_ref[d, keep:] = x_ref[inverse_ref[0, d], keep:]
        return carry

    lax.fori_loop(0, x_ref.shape[0], body, 0, unroll=8)


def split_kernel(x_ref, first_ref, rest_ref, sems):
    keep = first_ref.shape[1]
    copies = [
        pltpu.make_async_copy(x_ref.at[:, keep:], rest_ref, sems.at[0]),
        pltpu.make_async_copy(x_ref.at[:, :keep], first_ref, sems.at[1]),
    ]
    for copy in copies:
        copy.start()
    for copy in copies:
        copy.wait()


def shifted(x, distance):
    n = lax.axis_size("seq")
    return lax.ppermute(x, "seq", [(i, i + distance) for i in range(n) if 0 <= i + distance < n])


def swapped(x):
    return lax.ppermute(x, "seq", [(i, i ^ 1) for i in range(lax.axis_size("seq"))])


def exchange(x):
    groups = [list(range(core, lax.axis_size("seq"), 2)) for core in range(2)]
    return lax.all_to_all(x, "seq", 0, 0, axis_index_groups=groups, tiled=True)


def rows_last(x):
    return with_layout_constraint(x, Layout(tuple(range(x.ndim))))


def local(queries, keys, values, out_grad, route):
    q, k, v, g = queries[0], keys[0], values[0], out_grad[0]
    rows, width = q.shape
    n = lax.axis_size("seq")
    me = lax.axis_index("seq")
    factor = width**-0.5
    scale = factor * math.log2(math.e)
    at = me.reshape(1)
    places = n // 2
    part = 2 * rows // places
    swap = (route[0, 0] & 1) == 1
    block = jax.ShapeDtypeStruct((rows, width), BF16)

    vmem = pl.BlockSpec(memory_space=pltpu.VMEM)
    smem = pl.BlockSpec(memory_space=pltpu.SMEM)
    params = pltpu.CompilerParams(vmem_limit_bytes=VMEM_LIMIT)

    kv_own = jnp.concatenate([k, v])
    kv_before = shifted(kv_own, 1)
    kv_swapped = swapped(kv_own)

    def pairs(x):
        return x.reshape(-1, part // 2, 2, width)

    anywhere = pl.BlockSpec(memory_space=pl.ANY)
    own_stats = pl.pallas_call(
        functools.partial(own_kernel, scale),
        out_shape=jax.ShapeDtypeStruct((3, rows), F32),
        in_specs=[vmem] * 4,
        out_specs=vmem,
        compiler_params=params,
    )(q, g, k, v)
    stats, notes, spread = pl.pallas_call(
        functools.partial(stats_kernel, scale),
        out_shape=(
            jax.ShapeDtypeStruct((2, rows), F32),
            jax.ShapeDtypeStruct((places, width), BF16),
            jax.ShapeDtypeStruct((places, part + 1, 2, width), BF16),
        ),
        in_specs=[smem] * 2 + [vmem] * 4 + [anywhere] * 4,
        out_specs=(vmem, vmem, anywhere),
        scratch_shapes=[pltpu.VMEM((width, places), F32), pltpu.SemaphoreType.DMA((3,))],
        compiler_params=params,
    )(at, route.reshape(1), q, g, own_stats, kv_before, pairs(kv_own), pairs(kv_swapped), pairs(q), pairs(g))
    spread = spread.at[:, part].set(jnp.broadcast_to(notes[:, None], (places, 2, width)))
    spread = exchange(spread)
    square = jax.ShapeDtypeStruct((rows, rows), BF16)
    across32 = jax.ShapeDtypeStruct((width, rows), F32)
    from_local = pl.pallas_call(
        functools.partial(local_kernel, scale),
        out_shape=(across32,) * 3 + (square,) * 2 + (jax.ShapeDtypeStruct((width, rows), BF16),),
        in_specs=[smem] + [vmem] * 6,
        out_specs=(vmem,) * 6,
        compiler_params=params,
    )(at, q, g, k, v, kv_before, stats)
    qg_next, stats_next = shifted((jnp.concatenate([q, g]), stats), -1)
    spread, from_local, qg_next, stats_next = lax.optimization_barrier((spread, from_local, qg_next, stats_next))
    out, shaped_keys, weighted_keys, so, wo, g_t = from_local
    index = jax.ShapeDtypeStruct((1, places), jnp.int32)
    partner, inverse = call(partner_kernel, (index, index), 1)(spread[:, -1, 0])
    moved = call(reorder_kernel, jax.ShapeDtypeStruct(spread.shape, BF16), 1, 2)(partner, inverse, spread)
    moved = exchange(moved)
    from_next = pl.pallas_call(
        functools.partial(next_kernel, scale),
        out_shape=(square,) * 2,
        in_specs=[vmem] * 4,
        out_specs=(vmem,) * 2,
        compiler_params=params,
    )(qg_next, k, v, stats_next)
    moved, from_next = lax.optimization_barrier((moved, from_next))
    sn, wn = from_next
    kv, rest = pl.pallas_call(
        split_kernel,
        out_shape=(
            jax.ShapeDtypeStruct((places, part // 2, 2, width), BF16),
            jax.ShapeDtypeStruct((places, part // 2 + 1, 2, width), BF16),
        ),
        in_specs=[anywhere],
        out_specs=(vmem, vmem),
        scratch_shapes=[pltpu.SemaphoreType.DMA((2,))],
        compiler_params=params,
    )(moved)
    kv = kv.reshape(2 * rows, width)
    rest = rows_last(jnp.where(swap, swapped(rest), rest))
    qg = rest[:, : part // 2].reshape(2 * rows, width)
    notes = rest[:, -1, 0]

    attended, query_grad, shares = pl.pallas_call(
        functools.partial(query_kernel, scale, factor),
        out_shape=(block, block, jax.ShapeDtypeStruct((2, rows), F32)),
        in_specs=[vmem] * 8,
        out_specs=(vmem,) * 3,
        compiler_params=params,
    )(q, g, kv, stats, out, shaped_keys, weighted_keys, g_t)
    shares_next = shifted(shares, -1)
    dk, dv = pl.pallas_call(
        functools.partial(partner_terms_kernel, scale, factor),
        out_shape=(block, block),
        in_specs=[vmem] * 4,
        out_specs=(vmem,) * 2,
        scratch_shapes=[pltpu.VMEM((rows, rows), BF16)] * 2,
        compiler_params=params,
    )(qg, k, v, notes)
    one, two = pltpu.VMEM((rows, width), BF16), pltpu.VMEM((rows, 2 * width), BF16)
    key_grad, value_grad = pl.pallas_call(
        functools.partial(sum_kernel, factor),
        out_shape=(block, block),
        in_specs=[vmem] * 11,
        out_specs=(vmem,) * 2,
        scratch_shapes=[one, two, one, two],
        compiler_params=params,
    )(q, g, qg_next, shares, shares_next, so, wo, sn, wn, dk, dv)
    return attended[None], query_grad[None], key_grad[None], value_grad[None]


def solution(mesh):
    whole = P("head", "seq", None)
    return jax.shard_map(
        local,
        mesh=mesh,
        in_specs=(whole,) * 4 + (P("head", "seq"),),
        out_specs=(whole,) * 4,
        check_vma=False,
    )
```

```python
import functools
import math

import jax
import jax.numpy as jnp
from jax import lax
from jax.experimental import pallas as pl
from jax.experimental.layout import Layout, with_layout_constraint
from jax.experimental.pallas import tpu as pltpu
from jax.sharding import PartitionSpec as P

F32 = jnp.float32
BF16 = jnp.bfloat16
NT = (((1,), (1,)), ((), ()))
NN = (((1,), (0,)), ((), ()))
CHUNK = 256
MIDDLE = 512
LONG = 1024
INF = float("inf")
VMEM_LIMIT = 16 * 1024 * 1024


def dot(a, b, dims=NN):
    return lax.dot_general(a, b, dims, preferred_element_type=F32)


def chunks(rows, size=CHUNK):
    return [slice(at, at + size) for at in range(0, rows, size)]


def causal(scores, first):
    kpos = lax.broadcasted_iota(jnp.int32, scores.shape, 0)
    qpos = lax.broadcasted_iota(jnp.int32, scores.shape, 1) + first
    return jnp.where(kpos <= qpos, scores, -INF)


def call(kernel, out_shape, n_in, scalars=0):
    vmem = pl.BlockSpec(memory_space=pltpu.VMEM)
    smem = pl.BlockSpec(memory_space=pltpu.SMEM)
    return pl.pallas_call(
        kernel,
        out_shape=out_shape,
        in_specs=[smem] * scalars + [vmem] * n_in,
        out_specs=jax.tree.map(lambda _: vmem, out_shape),
        compiler_params=pltpu.CompilerParams(vmem_limit_bytes=VMEM_LIMIT),
    )


def thirds(x):
    high = x.astype(BF16).astype(F32)
    middle = (x - high).astype(BF16).astype(F32)
    return high, middle, x - high - middle


def own_kernel(scale, q_ref, g_ref, k_ref, v_ref, out_ref):
    for cols in chunks(q_ref.shape[0]):
        q, g = q_ref[cols], g_ref[cols]
        own = causal(dot(k_ref[: cols.stop], q, NT) * scale, cols.start)
        peak = jnp.max(own, 0, keepdims=True)
        own = jnp.exp2(own - peak)
        out_ref[0:1, cols] = peak
        out_ref[1:2, cols] = jnp.sum(own, 0, keepdims=True)
        out_ref[2:3, cols] = jnp.sum(own * dot(v_ref[: cols.stop], g, NT), 0, keepdims=True)


def stats_kernel(
    scale, at, route, q_ref, g_ref, own_ref, before_ref, own_pairs, swapped_pairs, q_pairs, g_pairs,
    out_ref, notes_ref, spread_ref, rows_ref, sems,
):
    leading = at[0] == 0
    half = own_pairs.shape[1]
    middle = q_pairs.shape[0]
    swap = route[0] & 1 == 1
    kv_to = spread_ref.at[:, :half]
    copies = [
        pltpu.make_async_copy(q_pairs, spread_ref.at[:middle, half : 2 * half], sems.at[0]),
        pltpu.make_async_copy(g_pairs, spread_ref.at[middle:, half : 2 * half], sems.at[1]),
    ]
    for copy in copies:
        copy.start()

    @pl.when(swap)
    def _():
        pltpu.make_async_copy(swapped_pairs, kv_to, sems.at[2]).start()

    @pl.when(jnp.logical_not(swap))
    def _():
        pltpu.make_async_copy(own_pairs, kv_to, sems.at[2]).start()

    rows = q_ref.shape[0]
    kb_ref, vb_ref = before_ref.at[:rows], before_ref.at[rows:]
    places = rows_ref.shape[1]
    parts = q_ref.shape[0] // places
    rows_ref[...] = jnp.full(rows_ref.shape, route[0].astype(F32))
    for cols in chunks(rows, MIDDLE):
        q, g = q_ref[cols], g_ref[cols]
        before = dot(kb_ref[...], q, NT) * scale
        peak_own = own_ref[0:1, cols]
        peak = jnp.maximum(peak_own, jnp.where(leading, -INF, jnp.max(before, 0, keepdims=True)))
        before = jnp.exp2(before - jnp.where(leading, INF, peak))
        share = jnp.exp2(peak_own - peak)
        total = share * own_ref[1:2, cols] + jnp.sum(before, 0, keepdims=True)
        pushed = share * own_ref[2:3, cols] + jnp.sum(before * dot(vb_ref[...], g, NT), 0, keepdims=True)
        for kind, row in enumerate((peak + jnp.log2(total), pushed / total)):
            out_ref[kind : kind + 1, cols] = row
            for i, third in enumerate(thirds(row)):
                for at_row in range(0, MIDDLE, places):
                    to = (3 * kind + i) * parts + (cols.start + at_row) // places
                    rows_ref[to : to + 1] = third[:, at_row : at_row + places]
    notes_ref[...] = rows_ref[...].T.astype(BF16)
    for copy in copies:
        copy.wait()
    pltpu.make_async_copy(own_pairs, kv_to, sems.at[2]).wait()


def read_notes(notes_ref, count):
    rows = notes_ref[...].astype(F32).T
    parts = count // rows.shape[1]
    per = parts * LONG // count
    sums = [sum(rows[(3 * kind + i) * parts : (3 * kind + i + 1) * parts] for i in range(3)) for kind in range(2)]
    return [
        [jnp.concatenate([total[t : t + 1] for t in range(at, at + per)], 1) for at in range(0, parts, per)]
        for total in sums
    ]


def joined(elsewhere, scores):
    peak = jnp.max(scores, 0, keepdims=True)
    raw = jnp.exp2(scores - peak)
    here = peak + jnp.log2(jnp.sum(raw, 0, keepdims=True))
    top = jnp.maximum(elsewhere, here)
    log_total = top + jnp.log2(jnp.exp2(elsewhere - top) + jnp.exp2(here - top))
    return raw * jnp.exp2(peak - log_total), log_total, jnp.exp2(elsewhere - log_total)


def local_kernel(
    scale, at, q_ref, g_ref, k_ref, v_ref, before_ref, stats_ref,
    out_ref, shaped_keys_ref, keys_ref, so_ref, wo_ref, g_t_ref,
):
    leading = at[0] == 0
    rows = k_ref.shape[0]
    kb_ref, vb_ref = before_ref.at[:rows], before_ref.at[rows:]
    g_t_ref[...] = g_ref[...].T
    k_t, kb_t = k_ref[...].T, kb_ref[...].T
    v_t, vb_t = v_ref[...].T, vb_ref[...].T
    for cols in chunks(q_ref.shape[0]):
        q, g = q_ref[cols], g_ref[cols]
        keys = slice(0, cols.stop)
        total, drift = stats_ref[0:1, cols], stats_ref[1:2, cols]

        def shape(weights, v):
            return (weights.astype(F32) * (dot(v, g, NT) - drift)).astype(BF16)

        wo = jnp.exp2(causal(dot(k_ref[keys], q, NT) * scale, cols.start) - total).astype(BF16)
        so = shape(wo, v_ref[keys])
        wb = jnp.exp2(dot(kb_ref[...], q, NT) * scale - jnp.where(leading, INF, total)).astype(BF16)
        sb = shape(wb, vb_ref[...])
        out_ref[:, cols] = dot(v_t[:, keys], wo) + dot(vb_t, wb)
        shaped_keys_ref[:, cols] = dot(k_t[:, keys], so) + dot(kb_t, sb)
        keys_ref[:, cols] = dot(k_t[:, keys], wo) + dot(kb_t, wb)
        wo_ref[keys, cols] = wo
        so_ref[keys, cols] = so


def next_kernel(scale, qg_ref, k_ref, v_ref, stats_ref, s_ref, w_ref):
    rows = k_ref.shape[0]
    q_ref, g_ref = qg_ref.at[:rows], qg_ref.at[rows:]
    for cols in chunks(rows):
        weights = jnp.exp2(dot(k_ref[...], q_ref[cols], NT) * scale - stats_ref[0:1, cols]).astype(BF16)
        pushed = dot(v_ref[...], g_ref[cols], NT)
        w_ref[:, cols] = weights
        s_ref[:, cols] = (weights.astype(F32) * (pushed - stats_ref[1:2, cols])).astype(BF16)


def scaled(q, g, shares_ref):
    down = jnp.concatenate([shares_ref[...]] * 4, 0).T
    share, delta = down[:, 0:1], down[:, 1:2]
    q, g = q.astype(F32), g.astype(F32)
    return (q * share).astype(BF16), jnp.concatenate([(q * delta).astype(BF16), (g * share).astype(BF16)], 1)


def query_kernel(
    scale, factor, q_ref, g_ref, partner_ref, stats_ref, out_ref, shaped_keys_ref, keys_ref, g_t_ref,
    att_ref, dq_ref, shares_ref,
):
    rows = q_ref.shape[0]
    kp_ref, vp_ref = partner_ref.at[:rows], partner_ref.at[rows:]
    kp_t, vp_t = kp_ref[...].T, vp_ref[...].T
    for cols in chunks(rows, LONG):
        q, g = q_ref[cols], g_ref[cols]
        weights, _, share = joined(stats_ref[0:1, cols], dot(kp_ref[...], q, NT) * scale)
        weights = weights.astype(BF16)
        attended = (dot(vp_t, weights) + share * out_ref[:, cols]).astype(BF16).astype(F32)
        att_ref[cols] = attended.T.astype(BF16)
        drift = jnp.sum(attended * g_t_ref[:, cols].astype(F32), 0, keepdims=True)
        delta = share * (stats_ref[1:2, cols] - drift)
        shaped = (weights.astype(F32) * (dot(vp_ref[...], g, NT) - drift)).astype(BF16)
        dq = dot(kp_t, shaped) + share * shaped_keys_ref[:, cols] + delta * keys_ref[:, cols]
        dq_ref[cols] = (dq * factor).T.astype(BF16)
        shares_ref[0:1, cols] = share
        shares_ref[1:2, cols] = delta


def partner_terms_kernel(scale, factor, qg_ref, k_ref, v_ref, notes_ref, _, dk_ref, dv_ref, s_ref, w_ref):
    rows = k_ref.shape[0]
    q_ref, g_ref = qg_ref.at[:rows], qg_ref.at[rows:]
    elsewhere, pushed_there = read_notes(notes_ref, rows)
    for t, cols in enumerate(chunks(rows, LONG)):
        q, g = q_ref[cols], g_ref[cols]
        weights, _, share = joined(elsewhere[t], dot(k_ref[...], q, NT) * scale)
        pushed = dot(v_ref[...], g, NT)
        drift = share * pushed_there[t] + jnp.sum(weights * pushed, 0, keepdims=True)
        weights = weights.astype(BF16)
        s_ref[:, cols] = (weights.astype(F32) * (pushed - drift)).astype(BF16)
        w_ref[:, cols] = weights
    dk_ref[...] = (dot(s_ref[...], q_ref[...]) * factor).astype(BF16)
    dv_ref[...] = dot(w_ref[...], g_ref[...]).astype(BF16)


def sum_kernel(
    factor, q_ref, g_ref, qg_next_ref, shares_ref, shares_next_ref, so_ref, wo_ref, sn_ref, wn_ref, dkp_ref, dvp_ref,
    dk_ref, dv_ref, key_x, both_x, next_key_x, next_both_x,
):
    rows, width = q_ref.shape
    key_x[...], both_x[...] = scaled(q_ref[...], g_ref[...], shares_ref)
    next_key_x[...], next_both_x[...] = scaled(qg_next_ref[:rows], qg_next_ref[rows:], shares_next_ref)
    for keys in chunks(rows):
        later = slice(keys.start, rows)
        both = dot(wn_ref[keys], next_both_x[...])
        dk = (dot(sn_ref[keys], next_key_x[...]) + both[:, :width]) * factor
        dk = dk.astype(BF16).astype(F32) + dkp_ref[keys].astype(F32)
        dv = both[:, width:].astype(BF16).astype(F32) + dvp_ref[keys].astype(F32)
        both = dot(wo_ref[keys, later], both_x[later])
        dk_ref[keys] = (dk + (dot(so_ref[keys, later], key_x[later]) + both[:, :width]) * factor).astype(BF16)
        dv_ref[keys] = (dv + both[:, width:]).astype(BF16)


def partner_kernel(notes_ref, partner_ref, inverse_ref):
    n = partner_ref.shape[1]
    route = (notes_ref[...].astype(F32).T[-1:]).astype(jnp.int32) >> 1
    lane = lax.broadcasted_iota(jnp.int32, route.shape, 1)

    def section(holder, s):
        far = 1 << s
        across = jnp.where((lane >> s) & 1 == 1, pltpu.roll(holder, far, 1), pltpu.roll(holder, n - far, 1))
        return jnp.where((route >> s) & 1 == 1, across, holder)

    sections = range(n.bit_length() - 1)
    partner_ref[...] = functools.reduce(section, sections, lane)
    inverse_ref[...] = functools.reduce(section, reversed(sections), lane)


def reorder_kernel(partner_ref, inverse_ref, x_ref, out_ref):
    keep = x_ref.shape[1] // 2

    def body(d, carry):
        out_ref[d, :keep] = x_ref[partner_ref[0, d], :keep]
        out_ref[d, keep:] = x_ref[inverse_ref[0, d], keep:]
        return carry

    lax.fori_loop(0, x_ref.shape[0], body, 0, unroll=8)


def split_kernel(x_ref, first_ref, rest_ref, sems):
    keep = first_ref.shape[1]
    copies = [
        pltpu.make_async_copy(x_ref.at[:, keep:], rest_ref, sems.at[0]),
        pltpu.make_async_copy(x_ref.at[:, :keep], first_ref, sems.at[1]),
    ]
    for copy in copies:
        copy.start()
    for copy in copies:
        copy.wait()


def shifted(x, distance):
    n = lax.axis_size("seq")
    return lax.ppermute(x, "seq", [(i, i + distance) for i in range(n) if 0 <= i + distance < n])


def swapped(x):
    return lax.ppermute(x, "seq", [(i, i ^ 1) for i in range(lax.axis_size("seq"))])


def exchange(x):
    groups = [list(range(core, lax.axis_size("seq"), 2)) for core in range(2)]
    return lax.all_to_all(x, "seq", 0, 0, axis_index_groups=groups, tiled=True)


def rows_last(x):
    return with_layout_constraint(x, Layout(tuple(range(x.ndim))))


def local(queries, keys, values, out_grad, route):
    q, k, v, g = queries[0], keys[0], values[0], out_grad[0]
    rows, width = q.shape
    n = lax.axis_size("seq")
    me = lax.axis_index("seq")
    factor = width**-0.5
    scale = factor * math.log2(math.e)
    at = me.reshape(1)
    places = n // 2
    part = 2 * rows // places
    swap = (route[0, 0] & 1) == 1
    block = jax.ShapeDtypeStruct((rows, width), BF16)

    vmem = pl.BlockSpec(memory_space=pltpu.VMEM)
    smem = pl.BlockSpec(memory_space=pltpu.SMEM)
    params = pltpu.CompilerParams(vmem_limit_bytes=VMEM_LIMIT)

    kv_own = jnp.concatenate([k, v])
    kv_before = shifted(kv_own, 1)
    kv_swapped = swapped(kv_own)

    def pairs(x):
        return x.reshape(-1, part // 2, 2, width)

    anywhere = pl.BlockSpec(memory_space=pl.ANY)
    own_stats = pl.pallas_call(
        functools.partial(own_kernel, scale),
        out_shape=jax.ShapeDtypeStruct((3, rows), F32),
        in_specs=[vmem] * 4,
        out_specs=vmem,
        compiler_params=params,
    )(q, g, k, v)
    stats, notes, spread = pl.pallas_call(
        functools.partial(stats_kernel, scale),
        out_shape=(
            jax.ShapeDtypeStruct((2, rows), F32),
            jax.ShapeDtypeStruct((places, width), BF16),
            jax.ShapeDtypeStruct((places, part + 1, 2, width), BF16),
        ),
        in_specs=[smem] * 2 + [vmem] * 4 + [anywhere] * 4,
        out_specs=(vmem, vmem, anywhere),
        scratch_shapes=[pltpu.VMEM((width, places), F32), pltpu.SemaphoreType.DMA((3,))],
        compiler_params=params,
    )(at, route.reshape(1), q, g, own_stats, kv_before, pairs(kv_own), pairs(kv_swapped), pairs(q), pairs(g))
    spread = spread.at[:, part].set(jnp.broadcast_to(notes[:, None], (places, 2, width)))
    spread = exchange(spread)
    square = jax.ShapeDtypeStruct((rows, rows), BF16)
    across32 = jax.ShapeDtypeStruct((width, rows), F32)
    from_local = pl.pallas_call(
        functools.partial(local_kernel, scale),
        out_shape=(across32,) * 3 + (square,) * 2 + (jax.ShapeDtypeStruct((width, rows), BF16),),
        in_specs=[smem] + [vmem] * 6,
        out_specs=(vmem,) * 6,
        compiler_params=params,
    )(at, q, g, k, v, kv_before, stats)
    qg_next, stats_next = shifted((jnp.concatenate([q, g]), stats), -1)
    spread, from_local, qg_next, stats_next = lax.optimization_barrier((spread, from_local, qg_next, stats_next))
    out, shaped_keys, weighted_keys, so, wo, g_t = from_local
    index = jax.ShapeDtypeStruct((1, places), jnp.int32)
    partner, inverse = call(partner_kernel, (index, index), 1)(spread[:, -1, 0])
    moved = call(reorder_kernel, jax.ShapeDtypeStruct(spread.shape, BF16), 1, 2)(partner, inverse, spread)
    moved = exchange(moved)
    from_next = pl.pallas_call(
        functools.partial(next_kernel, scale),
        out_shape=(square,) * 2,
        in_specs=[vmem] * 4,
        out_specs=(vmem,) * 2,
        compiler_params=params,
    )(qg_next, k, v, stats_next)
    moved, from_next = lax.optimization_barrier((moved, from_next))
    sn, wn = from_next
    kv, rest = pl.pallas_call(
        split_kernel,
        out_shape=(
            jax.ShapeDtypeStruct((places, part // 2, 2, width), BF16),
            jax.ShapeDtypeStruct((places, part // 2 + 1, 2, width), BF16),
        ),
        in_specs=[anywhere],
        out_specs=(vmem, vmem),
        scratch_shapes=[pltpu.SemaphoreType.DMA((2,))],
        compiler_params=params,
    )(moved)
    kv = kv.reshape(2 * rows, width)
    rest = rows_last(jnp.where(swap, swapped(rest), rest))
    qg = rest[:, : part // 2].reshape(2 * rows, width)
    notes = rest[:, -1, 0]

    attended, query_grad, shares = pl.pallas_call(
        functools.partial(query_kernel, scale, factor),
        out_shape=(block, block, jax.ShapeDtypeStruct((2, rows), F32)),
        in_specs=[vmem] * 8,
        out_specs=(vmem,) * 3,
        compiler_params=params,
    )(q, g, kv, stats, out, shaped_keys, weighted_keys, g_t)
    shares_next = shifted(shares, -1)
    dk, dv = pl.pallas_call(
        functools.partial(partner_terms_kernel, scale, factor),
        out_shape=(block, block),
        in_specs=[vmem] * 5,
        out_specs=(vmem,) * 2,
        scratch_shapes=[pltpu.VMEM((rows, rows), BF16)] * 2,
        compiler_params=params,
    )(qg, k, v, notes, wn)
    one, two = pltpu.VMEM((rows, width), BF16), pltpu.VMEM((rows, 2 * width), BF16)
    key_grad, value_grad = pl.pallas_call(
        functools.partial(sum_kernel, factor),
        out_shape=(block, block),
        in_specs=[vmem] * 11,
        out_specs=(vmem,) * 2,
        scratch_shapes=[one, two, one, two],
        compiler_params=params,
    )(q, g, qg_next, shares, shares_next, so, wo, sn, wn, dk, dv)
    return attended[None], query_grad[None], key_grad[None], value_grad[None]


def solution(mesh):
    whole = P("head", "seq", None)
    return jax.shard_map(
        local,
        mesh=mesh,
        in_specs=(whole,) * 4 + (P("head", "seq"),),
        out_specs=(whole,) * 4,
        check_vma=False,
    )
```
